128 devices in a mesh: dp: 4 (over x), fsdp: 32 (over z, y, core).
Axes of the slice: x: 4, y: 4, z: 4, core: 2. Of those that a mesh axis runs over, the one named last changes fastest.
Arguments:
- grad_parts: bfloat16 [4, 6144, 4096], P('dp', 'fsdp'), may hold values from -6 to 6
- weights: float32 [6144, 4096], P('fsdp', 'dp'), may hold values from -6 to 6
- moment_one: float32 [6144, 4096], P('fsdp', 'dp'), may hold values from -0.75 to 0.75
- moment_two: float32 [6144, 4096], P('fsdp', 'dp'), may hold values from 0.002 to 0.2
- left_basis: bfloat16 [6144, 6144], P('fsdp'), may hold values from -0.078125 to 0.078125
- right_basis: bfloat16 [4096, 4096], P(('dp', 'fsdp')), may hold values from -0.09375 to 0.09375
Outputs:
- new_weights: float32 [6144, 4096], P('fsdp', 'dp')
- new_one: float32 [6144, 4096], P('fsdp', 'dp')
- new_two: float32 [6144, 4096], P('fsdp', 'dp')
- update: float32 [6144, 4096], P('fsdp', 'dp')
The draws below stay inside these ranges and needn't reach their ends.
All inputs are finite; a program needn't handle non-finite values.
Results may differ from the reference program's by a relative error of at most 0.034.
Values may be sent and summed in bfloat16 or wider, within the bound.
No kernel may reach another device: no remote copies, remote signals or barrier semaphores. Data moves between devices by JAX's collectives and lax.ppermute only.
A program may use at most 128 MiB of HBM per device.

```python
import math
import jax
import jax.numpy as jnp
from jax import lax

M = 6144
N = 4096
N_DP = 4
N_FSDP = 32


def with_spikes(drawn, key, source, target, blocks, factor):
    def block_of(dim):
        return (jnp.arange(drawn.shape[dim]) // (drawn.shape[dim] // blocks)).reshape((-1,) + (1,) * (drawn.ndim - 1 - dim))

    near = jax.random.permutation(key, blocks)[block_of(target)]
    far = (block_of(target) + blocks // 2) % blocks
    return jnp.where((block_of(source) == near) | (block_of(source) == far), factor * drawn, drawn)


def shard_levels(own_key, extent, shards, smallest, high):
    factor_of, own = 1.0, jax.random.fold_in(own_key, 6)
    for axis_at, blocks in shards:
        draws = jnp.exp(jax.random.uniform(jax.random.fold_in(own, axis_at), (blocks,), jnp.float32, smallest / len(shards), high / len(shards)))
        factor_of = factor_of * jnp.repeat(draws, extent[axis_at] // blocks).reshape([-1 if axis == axis_at else 1 for axis in range(len(extent))])
    return factor_of


def bell_draw(key, extent, scale, most, cuts=(), kind=jnp.bfloat16):
    gain = shard_levels(key, extent, cuts, -0.22, 0.18) if cuts else 1.0
    values = jax.random.normal(key, extent, jnp.float32) * scale * gain
    return jnp.minimum(jnp.maximum(values, -most), most).astype(kind)


def bell_draw_with(key, dims, spread, limit, cuts, heavy, held_as=jnp.bfloat16):
    result = spread * jax.random.normal(key, dims, jnp.float32)
    if cuts:
        result = result * shard_levels(key, dims, cuts, -0.22, 0.18)
    return jnp.clip(with_spikes(result, jax.random.fold_in(key, 3), *heavy), -limit, limit).astype(held_as)


def setup_inputs(seed: int = 0) -> dict:
    key_list = jax.random.split(jax.random.key(seed), 7)
    return {
        "grad_parts": bell_draw_with(key_list[0], (N_DP, M, N), 0.5, 6.0, ((0, 4), (1, 32)), (0, 2, 4, 2.0)),
        "weights": bell_draw(key_list[1], (M, N), 1.0, 6.0, ((0, 32), (1, 4)), jnp.float32),
        "moment_one": bell_draw(key_list[2], (M, N), 0.05, 0.75, ((0, 32), (1, 4)), jnp.float32),
        "moment_two": jnp.clip(jnp.exp(math.log(0.2) - 4.6051702 * jax.random.uniform(key_list[3], (M, N), jnp.float32) ** shard_levels(key_list[3], (M, N), ((0, 32), (1, 4)), -0.2, 0.2)), 0.002, 0.2),
        "left_basis": bell_draw(key_list[4], (M, M), M ** -0.5, 0.078125, ((0, 32),)),
        "right_basis": bell_draw(key_list[5], (N, N), N ** -0.5, 0.09375, ((0, 128),)),
    }


beta_first = 0.95
beta_second = 0.95
bias_first = 1.0 - 0.95 ** 10
bias_second = 1.0 - 0.95 ** 10
epsilon = 1e-08
learn_rate = 0.02
weight_decay = 0.1

def reference(grad_parts, weights, moment_one, moment_two, left_basis, right_basis):
    gradient = lax.optimization_barrier(jnp.sum(grad_parts.astype(jnp.float32), axis=0)).astype(jnp.bfloat16)
    height = M // N_FSDP

    def left_add(index, total):
        first = (index * height).astype(jnp.int32)
        basis_rows = lax.dynamic_slice_in_dim(left_basis, first, height, 0)
        grad_rows = lax.dynamic_slice_in_dim(gradient, first, height, 0)
        piece = lax.dot_general(basis_rows, grad_rows, (((0,), (0,)), ((), ())), preferred_element_type=jnp.float32)
        piece = lax.optimization_barrier(piece.astype(jnp.bfloat16)).astype(jnp.float32)
        return total + piece
    summed = lax.fori_loop(0, N_FSDP, left_add, jnp.zeros((M, N), jnp.float32))
    rotated_left = summed.astype(jnp.bfloat16)
    width = N // N_DP
    rotated = jnp.zeros((M, N), jnp.float32)
    for block in range(N_DP):
        partial_sum = jnp.dot(rotated_left[:, block * width:(block + 1) * width], right_basis[block * width:(block + 1) * width, :], preferred_element_type=jnp.float32)
        rotated = rotated + lax.optimization_barrier(partial_sum.astype(jnp.bfloat16)).astype(jnp.float32)
    new_one = beta_first * moment_one + (1.0 - beta_first) * rotated
    new_two = beta_second * moment_two + (1.0 - beta_second) * rotated * rotated
    normed = (new_one / bias_first / (jnp.sqrt(new_two / bias_second) + epsilon)).astype(jnp.bfloat16)
    back_left = jnp.dot(left_basis, normed, preferred_element_type=jnp.float32).astype(jnp.bfloat16)
    update = lax.dot_general(back_left, right_basis, (((1,), (1,)), ((), ())), preferred_element_type=jnp.float32)
    new_weights = weights - learn_rate * (update + weight_decay * weights)
    return (new_weights, new_one, new_two, update)
```

```python
import jax
import jax.numpy as jnp
from jax import lax
from jax.sharding import Mesh, PartitionSpec as P

beta_first = 0.95
beta_second = 0.95
bias_first = 1.0 - 0.95**10
bias_second = 1.0 - 0.95**10
epsilon = 1e-08
learn_rate = 0.02
weight_decay = 0.1

RING = 4
bf16 = jnp.bfloat16
f32 = jnp.float32


def shift(value, axis, distance):
    return lax.ppermute(value, axis, [(i, (i + distance) % RING) for i in range(RING)])


def swap(value):
    return lax.ppermute(value, "core", [(0, 1), (1, 0)])


def dot(a, b, contract):
    return lax.dot_general(a, b, ((contract[:1], contract[1:]), ((), ())), preferred_element_type=f32)


def total(pieces):
    return sum(piece.astype(f32) for piece in pieces)


def per_device(grad_parts, weights, moment_one, moment_two, left_basis, right_basis):
    x, z, y, core = (lax.axis_index(name) for name in ("x", "z", "y", "core"))
    first = core == 0
    rows, features = left_basis.shape
    columns = weights.shape[1]
    half = columns // 2
    quarter = half // 2
    spread = features // RING
    chunk = 2 * rows

    def block(value, index, width):
        return lax.dynamic_slice_in_dim(value, (index % RING) * width, width, 1)

    whole = grad_parts[0]
    arrived = [shift(block(whole, x + d, columns), "x", d) for d in (1, 2, 3)]
    gradient = total([block(whole, x, columns), *arrived]).astype(bf16)
    both = jnp.concatenate([gradient, swap(gradient)], axis=0)

    by_core = right_basis.reshape(-1, RING, 2, half)
    mine = lax.dynamic_index_in_dim(by_core, core, 2, keepdims=False).reshape(-1, RING * half)
    others = lax.dynamic_index_in_dim(by_core, 1 - core, 2, keepdims=False).reshape(-1, RING * half)
    others = swap(others)
    pair = jnp.where(first, jnp.concatenate([mine, others]), jnp.concatenate([others, mine]))
    basis = lax.all_gather(pair, ("z", "y"), axis=0, tiled=True)

    by_y = left_basis.reshape(rows, RING, RING, chunk)

    def for_y(d):
        return lax.dynamic_index_in_dim(by_y, (y + d) % RING, 2, keepdims=False).reshape(rows, spread)

    left_y = jnp.concatenate([for_y(0)] + [shift(for_y(d), "y", d) for d in (1, 2, 3)])
    left_z = jnp.concatenate(
        [block(left_basis, z, spread)] + [shift(block(left_basis, z + d, spread), "z", d) for d in (1, 2, 3)]
    )
    left_y_other, left_z_other = swap(left_y), swap(left_z)

    parts = [dot(both, block(basis, x + d, half), (1, 0)).astype(bf16) for d in range(RING)]
    right = total([parts[0]] + [shift(parts[d], "x", d) for d in (1, 2, 3)]).astype(bf16)

    def rotate(value, left, left_other, axis, across, at):
        pieces = [value] + [shift(value, axis, d) for d in (1, 2, 3)]
        own = jnp.concatenate([p[:rows] for p in pieces])
        other = jnp.concatenate([p[rows:] for p in pieces])
        out = (dot(left, own, (0, 0)) + dot(left_other, other, (0, 0))).astype(bf16)

        def part(d):
            return lax.dynamic_slice_in_dim(out, ((at + d) % RING) * chunk, chunk, 0)

        return total([part(0)] + [shift(part(d), across, d) for d in (1, 2, 3)]).astype(bf16)

    turned = jnp.concatenate(
        [
            rotate(right[:, :quarter], left_y, left_y_other, "y", "z", z),
            rotate(right[:, quarter:], left_z, left_z_other, "z", "y", y),
        ],
        axis=1,
    )
    own = lax.dynamic_slice_in_dim(turned, core * rows, rows, 0)
    other = swap(lax.dynamic_slice_in_dim(turned, (1 - core) * rows, rows, 0))
    rotated = jnp.where(
        first, jnp.concatenate([own, other], axis=1), jnp.concatenate([other, own], axis=1)
    ).astype(f32)

    new_one = beta_first * moment_one + (1.0 - beta_first) * rotated
    new_two = beta_second * moment_two + (1.0 - beta_second) * rotated * rotated
    normed = (new_one / bias_first / (jnp.sqrt(new_two / bias_second) + epsilon)).astype(bf16)

    mine = lax.dynamic_slice_in_dim(normed, core * half, half, 1)
    others = swap(lax.dynamic_slice_in_dim(normed, (1 - core) * half, half, 1))
    normed = jnp.where(first, jnp.concatenate([mine, others]), jnp.concatenate([others, mine]))

    def back(value, left, left_other, axis, across, at):
        gathered = jnp.zeros((spread, quarter), bf16)
        for d in range(RING):
            piece = value if d == 0 else shift(value, across, d)
            gathered = lax.dynamic_update_slice_in_dim(gathered, piece, ((at - d) % RING) * chunk, 0)
        own = dot(left, gathered, (1, 0)).astype(bf16).reshape(RING, rows, quarter)
        other = dot(left_other, gathered, (1, 0)).astype(bf16).reshape(RING, rows, quarter)
        pieces = [jnp.concatenate([own[d], other[d]]) for d in range(RING)]
        return total([pieces[0]] + [shift(pieces[d], axis, -d) for d in (1, 2, 3)]).astype(bf16)

    back_left = jnp.concatenate(
        [
            back(normed[:, :quarter], left_y, left_y_other, "y", "z", z),
            back(normed[:, quarter:], left_z, left_z_other, "z", "y", y),
        ],
        axis=1,
    )

    update = dot(back_left, block(basis, x, half), (1, 1))
    for d in (1, 2, 3):
        update = update + dot(shift(back_left, "x", d), block(basis, x - d, half), (1, 1))
    update = update[:rows] + swap(update[rows:])
    new_weights = weights - learn_rate * (update + weight_decay * weights)
    return (new_weights, new_one, new_two, update)


def solution(mesh):
    grid = Mesh(mesh.devices.reshape(RING, RING, RING, 2), ("x", "z", "y", "core"))
    fsdp = ("z", "y", "core")
    placed = P(fsdp, "x")
    return jax.shard_map(
        per_device,
        mesh=grid,
        in_specs=(
            P("x", fsdp, None),
            placed,
            placed,
            placed,
            P(fsdp, None),
            P(("x", *fsdp), None),
        ),
        out_specs=(placed, placed, placed, placed),
        check_vma=False,
    )
```

```python
import jax
import jax.numpy as jnp
from jax import lax
from jax.experimental import pallas as pl
from jax.experimental.pallas import tpu as pltpu
from jax.sharding import Mesh, PartitionSpec as P

beta_first = 0.95
beta_second = 0.95
bias_first = 1.0 - 0.95**10
bias_second = 1.0 - 0.95**10
epsilon = 1e-08
learn_rate = 0.02
weight_decay = 0.1

RING = 4
CHUNKS = 2
bf16 = jnp.bfloat16
f32 = jnp.float32
VMEM_LIMIT = 40 * 1024 * 1024


def shift(value, axis, distance):
    return lax.ppermute(value, axis, [(i, (i + distance) % RING) for i in range(RING)])


def swap(value):
    return lax.ppermute(value, "core", [(0, 1), (1, 0)])


def total(pieces):
    return sum(piece.astype(f32) for piece in pieces)


def call(kernel, place, operands, outs, flops, scratch=()):
    moved = sum(a.size * a.dtype.itemsize for a in operands)
    moved += sum(s.size * jnp.dtype(s.dtype).itemsize for s in outs)
    return pl.pallas_call(
        kernel,
        out_shape=outs,
        in_specs=[pl.BlockSpec(memory_space=pltpu.SMEM)]
        + [pl.BlockSpec(memory_space=pltpu.VMEM)] * len(operands),
        out_specs=[pl.BlockSpec(memory_space=pltpu.VMEM)] * len(outs),
        scratch_shapes=list(scratch),
        cost_estimate=pl.CostEstimate(flops=flops, bytes_accessed=moved, transcendentals=0),
        compiler_params=pltpu.CompilerParams(vmem_limit_bytes=VMEM_LIMIT),
    )(place, *operands)


def at(index, width):
    return pl.ds(pl.multiple_of(lax.rem(index + RING, RING) * width, width), width)


def right_kernel(place, own, other, here, before, after, far_low, far_high, *refs):
    outs, basis, grad = refs[:RING], refs[RING], refs[RING + 1]
    x, z = place[0], place[1]
    rows, depth = own.shape[0], here.shape[0]
    grad[:rows] = own[...]
    grad[rows:] = other[...]
    basis[at(z, depth)] = here[...]
    basis[at(z - 1, depth)] = before[...]
    basis[at(z + 1, depth)] = after[...]
    start = lax.rem(z + 2, RING) * depth
    basis[pl.ds(pl.multiple_of(start, depth), depth // 2)] = far_low[...]
    basis[pl.ds(pl.multiple_of(start + depth // 2, depth // 2), depth // 2)] = far_high[...]
    width = outs[0].shape[1]
    for d in range(RING):
        outs[d][...] = jnp.dot(
            grad[...], basis[:, at(x + d, width)], preferred_element_type=f32
        ).astype(bf16)


def left_kernel(place, *refs):
    pieces, left, left_other = refs[:RING], refs[RING], refs[RING + 1]
    outs, stack, stack_other = refs[RING + 2 : 2 * RING + 2], refs[-2], refs[-1]
    y, z = place[2], place[1]
    rows = pieces[0].shape[0] // 2
    for d in range(RING):
        stack[at(y - d, rows)] = pieces[d][:rows]
        stack_other[at(y - d, rows)] = pieces[d][rows:]
    chunk = outs[0].shape[0]
    over = (((0,), (0,)), ((), ()))
    for d in range(RING):
        columns = at(z + d, chunk)
        value = lax.dot_general(stack[...], left[:, columns], over, preferred_element_type=f32)
        value += lax.dot_general(
            stack_other[...], left_other[:, columns], over, preferred_element_type=f32
        )
        outs[d][...] = value.T.astype(bf16)


def back_kernel(place, *refs):
    pieces, left, left_other = refs[:RING], refs[RING], refs[RING + 1]
    outs, stack = refs[RING + 2 : 2 * RING + 2], refs[-1]
    y, z, core = place[2], place[1], place[3]
    chunk = pieces[0].shape[0]
    rows = chunk // 2
    for d in range(RING):
        start = lax.rem(z - d + RING, RING) * chunk
        stack[pl.ds(pl.multiple_of(start + core * rows, rows), rows)] = pieces[d][:rows]
        stack[pl.ds(pl.multiple_of(start + (1 - core) * rows, rows), rows)] = pieces[d][rows:]
    for d in range(RING):
        lines = at(y - d, rows)
        outs[d][:rows] = jnp.dot(left[lines], stack[...], preferred_element_type=f32).astype(bf16)
        outs[d][rows:] = jnp.dot(
            left_other[lines], stack[...], preferred_element_type=f32
        ).astype(bf16)


def final_kernel(place, *refs):
    pieces, basis = refs[:RING], refs[RING]
    so_far, (own, other) = refs[RING + 1 : -2], refs[-2:]
    x = place[0]
    rows, width = own.shape[0], pieces[0].shape[1]
    over = (((1,), (1,)), ((), ()))
    value = sum(
        lax.dot_general(pieces[d][...], basis[:, at(x - d, width)], over, preferred_element_type=f32)
        for d in range(RING)
    )
    if so_far:
        own[...] = so_far[0][...] + value[:rows]
        other[...] = so_far[1][...] + value[rows:]
    else:
        own[...] = value[:rows]
        other[...] = value[rows:]


def moment_kernel(place, own, other, one, two, *refs):
    new_one, new_two, normed = refs[-3:]
    step = pl.program_id(0)
    rotated = jnp.where(step == 0, own[...].astype(f32), other[...].astype(f32))
    first = beta_first * one[...] + (1.0 - beta_first) * rotated
    second = beta_second * two[...] + (1.0 - beta_second) * rotated * rotated
    new_one[...] = first
    new_two[...] = second
    normed[0] = (first / bias_first / (jnp.sqrt(second / bias_second) + epsilon)).astype(bf16)


def moments(place, chunk, own, other, one, two, so_far):
    rows, width = own.shape

    def block(step, place):
        return (0, lax.rem(place[3] + step, 2) * CHUNKS + chunk)

    whole = pl.BlockSpec((rows, width), lambda step, place: (0, 0))
    part = pl.BlockSpec((rows, width), block)
    like = jax.ShapeDtypeStruct(one.shape, f32)
    kept = [pl.BlockSpec(memory_space=pl.ANY)] * len(so_far)
    return pl.pallas_call(
        moment_kernel,
        out_shape=[like, like, jax.ShapeDtypeStruct((2, rows, width), bf16)],
        grid_spec=pltpu.PrefetchScalarGridSpec(
            num_scalar_prefetch=1,
            grid=(2,),
            in_specs=[whole, whole, part, part, *kept],
            out_specs=[part, part, pl.BlockSpec((1, rows, width), lambda step, place: (step, 0, 0))],
        ),
        input_output_aliases={5: 0, 6: 1} if so_far else {},
        cost_estimate=pl.CostEstimate(flops=rows * width * 30, bytes_accessed=rows * width * 40, transcendentals=0),
        compiler_params=pltpu.CompilerParams(vmem_limit_bytes=VMEM_LIMIT),
    )(place, own, other, one, two, *so_far)


def per_device(grad_parts, weights, moment_one, moment_two, left_basis, right_basis):
    x, z, y, core = (lax.axis_index(name) for name in ("x", "z", "y", "core"))
    place = jnp.stack([x, z, y, core]).astype(jnp.int32)
    first = core == 0
    rows, features = left_basis.shape
    columns = weights.shape[1]
    half = columns // 2
    width = half // CHUNKS
    spread = features // RING
    both = 2 * rows

    def of_core(value, which):
        return jnp.concatenate(
            [value[:, (2 * k + which) * half : (2 * k + which + 1) * half] for k in range(RING)], axis=1
        )

    zero, one = of_core(right_basis, 0), of_core(right_basis, 1)
    arrived = swap(jnp.where(first, one, zero))
    pair = jnp.where(first, jnp.concatenate([zero, arrived]), jnp.concatenate([arrived, one]))
    lines = [pair] + [shift(pair, "y", d) for d in (1, 2, 3)]
    turned = jnp.stack(lines)
    by_y = jnp.concatenate(
        [lax.dynamic_index_in_dim(turned, (y - k) % RING, 0, keepdims=False) for k in range(RING)]
    )

    split = jnp.stack([grad_parts[0][:, k * columns : (k + 1) * columns] for k in range(RING)])
    gradient = total(list(lax.all_to_all(split, "x", 0, 0, tiled=True))).astype(bf16)
    gradient_other = swap(gradient)

    split = jnp.stack(
        [
            jnp.concatenate(
                [left_basis[:, j * spread + k * both : j * spread + (k + 1) * both] for j in range(RING)], axis=1
            )
            for k in range(RING)
        ]
    )
    left = lax.all_to_all(split, "y", 0, 0, tiled=True).reshape(RING * rows, spread)
    left_other = swap(left)

    bases, values = [], []
    for chunk in range(CHUNKS):
        here = jnp.concatenate(
            [by_y[:, k * half + chunk * width : k * half + (chunk + 1) * width] for k in range(RING)], axis=1
        )
        middle = here.shape[0] // 2
        before, after = shift(here, "z", 1), shift(here, "z", -1)
        low, high = shift(before[:middle], "z", 1), shift(after[middle:], "z", -1)
        piece = jax.ShapeDtypeStruct((both, width), bf16)
        *parts, basis = call(
            right_kernel,
            place,
            [gradient, gradient_other, here, before, after, low, high],
            [piece] * RING + [jax.ShapeDtypeStruct((columns, RING * width), bf16)],
            2 * both * columns * RING * width,
            [pltpu.VMEM((both, columns), bf16)],
        )
        bases.append(basis)
        values.append(total([parts[0]] + [shift(parts[d], "x", d) for d in (1, 2, 3)]).astype(bf16))

    sums = []
    for value in values:
        pieces = [value] + [shift(value, "y", d) for d in (1, 2, 3)]
        parts = call(
            left_kernel,
            place,
            [*pieces, left, left_other],
            [jax.ShapeDtypeStruct((both, width), bf16)] * RING,
            2 * 2 * left.size * width,
            [pltpu.VMEM((RING * rows, width), bf16)] * 2,
        )
        sums.append(total([parts[0]] + [shift(parts[d], "z", d) for d in (1, 2, 3)]).astype(bf16))

    so_far, normed = (), []
    for chunk, value in enumerate(sums):
        upper, lower = value[:rows], value[rows:]
        own = jnp.where(first, upper, lower)
        other = swap(jnp.where(first, lower, upper))
        *so_far, scaled = moments(place, chunk, own, other, moment_one, moment_two, so_far)
        normed.append(jnp.concatenate([scaled[0], swap(scaled[1])]))
    new_one, new_two = so_far

    backs = []
    for value in normed:
        pieces = [value] + [shift(value, "z", d) for d in (1, 2, 3)]
        parts = call(
            back_kernel,
            place,
            [*pieces, left, left_other],
            [jax.ShapeDtypeStruct((both, width), bf16)] * RING,
            2 * 2 * left.size * width,
            [pltpu.VMEM((spread, width), bf16)],
        )
        backs.append(total([parts[0]] + [shift(parts[d], "y", -d) for d in (1, 2, 3)]).astype(bf16))

    so_far = []
    for value, basis in zip(backs, bases):
        pieces = [value] + [shift(value, "x", d) for d in (1, 2, 3)]
        so_far = call(
            final_kernel,
            place,
            [*pieces, basis, *so_far],
            [jax.ShapeDtypeStruct((rows, columns), f32)] * 2,
            2 * both * columns * RING * width,
        )
    update = so_far[0] + swap(so_far[1])
    new_weights = weights - learn_rate * (update + weight_decay * weights)
    return (new_weights, new_one, new_two, update)


def solution(mesh):
    grid = Mesh(mesh.devices.reshape(RING, RING, RING, 2), ("x", "z", "y", "core"))
    fsdp = ("z", "y", "core")
    placed = P(fsdp, "x")
    return jax.shard_map(
        per_device,
        mesh=grid,
        in_specs=(
            P("x", fsdp, None),
            placed,
            placed,
            placed,
            P(fsdp, None),
            P(("x", *fsdp), None),
        ),
        out_specs=(placed, placed, placed, placed),
        check_vma=False,
    )
```

```python
import functools

import jax
import jax.numpy as jnp
from jax import lax
from jax.experimental import pallas as pl
from jax.experimental.pallas import tpu as pltpu
from jax.sharding import Mesh, PartitionSpec as P

beta_first = 0.95
beta_second = 0.95
bias_first = 1.0 - 0.95**10
bias_second = 1.0 - 0.95**10
epsilon = 1e-08
learn_rate = 0.02
weight_decay = 0.1

RING = 4
CHUNKS = 2
bf16 = jnp.bfloat16
f32 = jnp.float32
VMEM_LIMIT = 40 * 1024 * 1024


def shift(value, axis, distance):
    return lax.ppermute(value, axis, [(i, (i + distance) % RING) for i in range(RING)])


def swap(value):
    return lax.ppermute(value, "core", [(0, 1), (1, 0)])


def gather(value, axis):
    return [value] + [shift(value, axis, d) for d in (1, 2, 3)]


def spread(parts, axis, sign=1):
    return [parts[0]] + [shift(parts[d], axis, sign * d) for d in (1, 2, 3)]


def shape(rows, columns, kind=bf16):
    return jax.ShapeDtypeStruct((rows, columns), kind)


def call(kernel, place, operands, outs, flops=0, scratch=(), after=()):
    def body(place, *refs):
        kernel(place, *refs[: len(operands)], *refs[len(operands) + len(after) :])

    moved = sum(a.size * a.dtype.itemsize for a in operands)
    moved += sum(s.size * jnp.dtype(s.dtype).itemsize for s in outs)
    return pl.pallas_call(
        body,
        out_shape=outs,
        in_specs=[pl.BlockSpec(memory_space=pltpu.SMEM)]
        + [pl.BlockSpec(memory_space=pltpu.VMEM)] * len(operands)
        + [pl.BlockSpec(memory_space=pl.ANY)] * len(after),
        out_specs=[pl.BlockSpec(memory_space=pltpu.VMEM)] * len(outs),
        scratch_shapes=list(scratch),
        cost_estimate=pl.CostEstimate(flops=flops, bytes_accessed=moved, transcendentals=0),
        compiler_params=pltpu.CompilerParams(vmem_limit_bytes=VMEM_LIMIT),
    )(place, *operands, *after)


def at(index, width):
    return pl.ds(pl.multiple_of(lax.rem(index + RING, RING) * width, width), width)


def side(which, width):
    return pl.ds(pl.multiple_of(which * width, width), width)


def strips_kernel(place, value, out):
    width = out.shape[2] // RING
    for k in range(RING):
        for j in range(RING):
            start = (j * RING + k) * width
            out[k, :, j * width : (j + 1) * width] = value[:, start : start + width]


def lend_kernel(place, value, out):
    out[...] = value[:, side(1 - place[3], out.shape[1])]


def join_kernel(place, value, arrived, *outs):
    rows, width = value.shape[0], outs[0].shape[1]
    for chunk, out in enumerate(outs):
        out[:rows] = value[:, side(place[3] * CHUNKS + chunk, width)]
        out[rows:] = arrived[:, chunk * width : (chunk + 1) * width]


def stack_kernel(place, own, arrived, out):
    rows = own.shape[0]
    out[side(place[3], rows)] = own[...]
    out[side(1 - place[3], rows)] = arrived[...]


def left_kernel(place, *refs):
    pieces, left, left_other = refs[:RING], refs[RING], refs[RING + 1]
    outs, stack, stack_other = refs[RING + 2 : 2 * RING + 2], refs[-2], refs[-1]
    rows, chunk = pieces[0].shape[0] // 2, outs[0].shape[0]
    for d in range(RING):
        stack[at(place[2] - d, rows)] = pieces[d][:rows]
        stack_other[at(place[2] - d, rows)] = pieces[d][rows:]
    over = (((0,), (0,)), ((), ()))
    for d in range(RING):
        columns = at(place[1] + d, chunk)
        value = lax.dot_general(stack[...], left[:, columns], over, preferred_element_type=f32)
        value += lax.dot_general(
            stack_other[...], left_other[:, columns], over, preferred_element_type=f32
        )
        outs[d][...] = value.T.astype(bf16)


def sum_kernel(absolute, place, *refs):
    pieces, own, other = refs[:RING], refs[RING], refs[RING + 1]
    rows = own.shape[0]
    for k, out in enumerate((own, other)):
        which = k + place[3] * (1 - 2 * k) if absolute else k
        lines = side(which, rows) if absolute else slice(k * rows, (k + 1) * rows)
        out[...] = sum(piece[lines].astype(f32) for piece in pieces).astype(bf16)


def right_kernel(place, *refs):
    own, arrived, basis = refs[:CHUNKS], refs[CHUNKS : 2 * CHUNKS], refs[2 * CHUNKS]
    outs, rows = refs[2 * CHUNKS + 1 : -1], refs[-1]
    width = own[0].shape[1]
    for chunk in range(CHUNKS):
        rows[:, side(place[3] * CHUNKS + chunk, width)] = own[chunk][...]
        rows[:, side((1 - place[3]) * CHUNKS + chunk, width)] = arrived[chunk][...]
    for chunk in range(CHUNKS):
        for d in range(RING):
            for core in range(2):
                block = (lax.rem(place[0] + d, RING) * 2 + core) * CHUNKS + chunk
                outs[chunk * RING + d][:, core * width : (core + 1) * width] = jnp.dot(
                    rows[...], basis[:, side(block, width)], preferred_element_type=f32
                ).astype(bf16)


def moment_kernel(place, *refs):
    pieces, one, two = refs[:RING], refs[RING], refs[RING + 1]
    new_one, new_two, kept, lent = refs[-4:]
    core = pl.program_id(0)
    rotated = sum(piece[...].astype(f32) for piece in pieces)
    first = beta_first * one[...] + (1.0 - beta_first) * rotated
    second = beta_second * two[...] + (1.0 - beta_second) * rotated * rotated
    new_one[...] = first
    new_two[...] = second
    normed = (first / bias_first / (jnp.sqrt(second / bias_second) + epsilon)).astype(bf16)

    @pl.when(core == place[3])
    def _():
        kept[...] = normed

    @pl.when(core != place[3])
    def _():
        lent[...] = normed


def moments(place, chunk, pieces, one, two, so_far):
    rows, width = pieces[0].shape[0], pieces[0].shape[1] // 2
    piece = pl.BlockSpec((rows, width), lambda core, place: (0, core))
    part = pl.BlockSpec((rows, width), lambda core, place: (0, core * CHUNKS + chunk))
    whole = pl.BlockSpec((rows, width), lambda core, place: (0, 0))
    return pl.pallas_call(
        moment_kernel,
        out_shape=[shape(*one.shape, f32)] * 2 + [shape(rows, width)] * 2,
        grid_spec=pltpu.PrefetchScalarGridSpec(
            num_scalar_prefetch=1,
            grid=(2,),
            in_specs=[piece] * RING + [part, part] + [pl.BlockSpec(memory_space=pl.ANY)] * len(so_far),
            out_specs=[part, part, whole, whole],
        ),
        input_output_aliases={RING + 3: 0, RING + 4: 1} if so_far else {},
        compiler_params=pltpu.CompilerParams(vmem_limit_bytes=VMEM_LIMIT),
    )(place, *pieces, one, two, *so_far)


def back_kernel(place, *refs):
    pieces, left, left_other = refs[:RING], refs[RING], refs[RING + 1]
    outs, stack = refs[RING + 2 : 2 * RING + 2], refs[-1]
    chunk = pieces[0].shape[0]
    rows = chunk // 2
    for d in range(RING):
        stack[at(place[1] - d, chunk)] = pieces[d][...]
    for d in range(RING):
        lines = at(place[2] - d, rows)
        outs[d][:rows] = jnp.dot(left[lines], stack[...], preferred_element_type=f32).astype(bf16)
        outs[d][rows:] = jnp.dot(
            left_other[lines], stack[...], preferred_element_type=f32
        ).astype(bf16)


def beside_kernel(place, own, arrived, out):
    width = own.shape[1]
    out[:, side(place[3], width)] = own[...]
    out[:, side(1 - place[3], width)] = arrived[...]


def final_kernel(chunk, place, *refs):
    pieces, basis = refs[:RING], refs[RING]
    width = pieces[0].shape[1] // 2
    over = (((1,), (1,)), ((), ()))
    value = None
    for d in range(RING):
        for core in range(2):
            block = (lax.rem(place[0] - d + RING, RING) * 2 + core) * CHUNKS + chunk
            term = lax.dot_general(
                pieces[d][:, core * width : (core + 1) * width],
                basis[:, side(block, width)],
                over,
                preferred_element_type=f32,
            )
            value = term if value is None else value + term
    rest = refs[RING + 1 :]
    if chunk > 0:
        value = value + rest[0][...]
        rest = rest[1:]
    if chunk == CHUNKS - 1:
        weights, new_weights, update = rest
        update[...] = value
        new_weights[...] = weights[...] - learn_rate * (value + weight_decay * weights[...])
    else:
        rest[0][...] = value


def per_device(grad_parts, weights, moment_one, moment_two, left_basis, right_basis):
    place = jnp.stack([lax.axis_index(name) for name in ("x", "z", "y", "core")]).astype(jnp.int32)
    rows, features = left_basis.shape
    columns = weights.shape[1]
    half = columns // 2
    width = half // CHUNKS
    strip = features // RING
    both = 2 * rows

    (parts,) = call(strips_kernel, place, [left_basis], [jax.ShapeDtypeStruct((RING, rows, strip), bf16)])
    left = lax.all_to_all(parts, "y", 0, 0, tiled=True).reshape(RING * rows, strip)
    left_other = swap(left)

    gradient = lax.psum_scatter(grad_parts[0], "x", scatter_dimension=1, tiled=True)
    (lent,) = call(lend_kernel, place, [gradient], [shape(rows, half)])
    chunks = call(
        join_kernel, place, [gradient, swap(lent)], [shape(both, width)] * CHUNKS
    )
    basis = lax.all_gather(right_basis, ("z", "y", "core"), axis=0, tiled=True)

    kept, arrived = [], []
    for value in chunks:
        parts = call(
            left_kernel,
            place,
            [*gather(value, "y"), left, left_other],
            [shape(both, width)] * RING,
            4 * left.size * width,
            [pltpu.VMEM((RING * rows, width), bf16)] * 2,
        )
        own, other = call(
            functools.partial(sum_kernel, True), place, spread(parts, "z"), [shape(rows, width)] * 2
        )
        kept.append(own)
        arrived.append(swap(other))

    parts = call(
        right_kernel,
        place,
        [*kept, *arrived, basis],
        [shape(rows, 2 * width)] * (RING * CHUNKS),
        2 * rows * columns * RING * columns,
        [pltpu.VMEM((rows, columns), bf16)],
    )
    so_far, chunks = (), []
    for chunk in range(CHUNKS):
        pieces = spread(parts[chunk * RING : (chunk + 1) * RING], "x")
        *so_far, own, lent = moments(place, chunk, pieces, moment_one, moment_two, so_far)
        chunks.append(call(stack_kernel, place, [own, swap(lent)], [shape(both, width)])[0])
    new_one, new_two = so_far

    so_far = []
    for chunk, value in enumerate(chunks):
        parts = call(
            back_kernel,
            place,
            [*gather(value, "z"), left, left_other],
            [shape(both, width)] * RING,
            4 * left.size * width,
            [pltpu.VMEM((strip, width), bf16)],
        )
        own, other = call(
            functools.partial(sum_kernel, False), place, spread(parts, "y", -1), [shape(rows, width)] * 2
        )
        (value,) = call(beside_kernel, place, [own, swap(other)], [shape(rows, 2 * width)])
        last = chunk == CHUNKS - 1
        so_far = call(
            functools.partial(final_kernel, chunk),
            place,
            [*gather(value, "x"), basis, *so_far, *([weights] if last else [])],
            [shape(rows, columns, f32)] * (2 if last else 1),
            2 * rows * basis.size // CHUNKS,
        )
    new_weights, update = so_far
    return (new_weights, new_one, new_two, update)


def solution(mesh):
    grid = Mesh(mesh.devices.reshape(RING, RING, RING, 2), ("x", "z", "y", "core"))
    fsdp = ("z", "y", "core")
    placed = P(fsdp, "x")
    return jax.shard_map(
        per_device,
        mesh=grid,
        in_specs=(
            P("x", fsdp, None),
            placed,
            placed,
            placed,
            P(fsdp, None),
            P(("x", *fsdp), None),
        ),
        out_specs=(placed, placed, placed, placed),
        check_vma=False,
    )
```

```python
import functools

import jax
import jax.numpy as jnp
from jax import lax
from jax.experimental import pallas as pl
from jax.experimental.pallas import tpu as pltpu
from jax.sharding import Mesh, PartitionSpec as P

beta_first = 0.95
beta_second = 0.95
bias_first = 1.0 - 0.95**10
bias_second = 1.0 - 0.95**10
epsilon = 1e-08
learn_rate = 0.02
weight_decay = 0.1

RING = 4
CHUNKS = 2
bf16 = jnp.bfloat16
f32 = jnp.float32
VMEM_LIMIT = 40 * 1024 * 1024


def shift(value, axis, distance):
    return lax.ppermute(value, axis, [(i, (i + distance) % RING) for i in range(RING)])


def swap(value):
    return lax.ppermute(value, "core", [(0, 1), (1, 0)])


def gather(value, axis):
    return [value] + [shift(value, axis, d) for d in (1, 2, 3)]


def spread(parts, axis, sign=1):
    return [parts[0]] + [shift(parts[d], axis, sign * d) for d in (1, 2, 3)]


def shape(rows, columns, kind=bf16):
    return jax.ShapeDtypeStruct((rows, columns), kind)


def call(kernel, place, operands, outs, flops=0, scratch=(), after=()):
    def body(place, *refs):
        kernel(place, *refs[: len(operands)], *refs[len(operands) + len(after) :])

    moved = sum(a.size * a.dtype.itemsize for a in operands)
    moved += sum(s.size * jnp.dtype(s.dtype).itemsize for s in outs)
    return pl.pallas_call(
        body,
        out_shape=outs,
        in_specs=[pl.BlockSpec(memory_space=pltpu.SMEM)]
        + [pl.BlockSpec(memory_space=pltpu.VMEM)] * len(operands)
        + [pl.BlockSpec(memory_space=pl.ANY)] * len(after),
        out_specs=[pl.BlockSpec(memory_space=pltpu.VMEM)] * len(outs),
        scratch_shapes=list(scratch),
        cost_estimate=pl.CostEstimate(flops=flops, bytes_accessed=moved, transcendentals=0),
        compiler_params=pltpu.CompilerParams(vmem_limit_bytes=VMEM_LIMIT),
    )(place, *operands, *after)


def at(index, width):
    return pl.ds(pl.multiple_of(lax.rem(index + RING, RING) * width, width), width)


def side(which, width):
    return pl.ds(pl.multiple_of(which * width, width), width)


def strips_kernel(place, value, out):
    width = out.shape[2] // RING
    for k in range(RING):
        for j in range(RING):
            start = (j * RING + k) * width
            out[k, :, j * width : (j + 1) * width] = value[:, start : start + width]


def held(value, after):
    return pl.pallas_call(
        lambda *refs: None,
        out_shape=jax.ShapeDtypeStruct(value.shape, value.dtype),
        in_specs=[pl.BlockSpec(memory_space=pl.ANY)] * (1 + len(after)),
        out_specs=pl.BlockSpec(memory_space=pl.ANY),
        input_output_aliases={0: 0},
    )(value, *after)


def lend_kernel(place, value, out):
    out[...] = value[:, side(1 - place[3], out.shape[1])]


def join_kernel(place, value, arrived, *outs):
    rows, width = value.shape[0], outs[0].shape[1]
    for chunk, out in enumerate(outs):
        out[:rows] = value[:, side(place[3] * CHUNKS + chunk, width)]
        out[rows:] = arrived[:, chunk * width : (chunk + 1) * width]


def stack_kernel(place, own, arrived, out):
    rows = own.shape[0]
    out[side(place[3], rows)] = own[...]
    out[side(1 - place[3], rows)] = arrived[...]


def left_kernel(place, *refs):
    pieces, left, left_other = refs[:RING], refs[RING], refs[RING + 1]
    outs, stack, stack_other = refs[RING + 2 : 2 * RING + 2], refs[-2], refs[-1]
    rows, chunk = pieces[0].shape[0] // 2, outs[0].shape[0]
    for d in range(RING):
        stack[at(place[2] - d, rows)] = pieces[d][:rows]
        stack_other[at(place[2] - d, rows)] = pieces[d][rows:]
    over = (((0,), (0,)), ((), ()))
    for d in range(RING):
        columns = at(place[1] + d, chunk)
        value = lax.dot_general(stack[...], left[:, columns], over, preferred_element_type=f32)
        value += lax.dot_general(
            stack_other[...], left_other[:, columns], over, preferred_element_type=f32
        )
        outs[d][...] = value.T.astype(bf16)


def sum_kernel(absolute, place, *refs):
    pieces, own, other = refs[:RING], refs[RING], refs[RING + 1]
    rows = own.shape[0]
    for k, out in enumerate((own, other)):
        which = k + place[3] * (1 - 2 * k) if absolute else k
        lines = side(which, rows) if absolute else slice(k * rows, (k + 1) * rows)
        out[...] = sum(piece[lines].astype(f32) for piece in pieces).astype(bf16)


def right_kernel(place, *refs):
    own, arrived, basis = refs[:CHUNKS], refs[CHUNKS : 2 * CHUNKS], refs[2 * CHUNKS]
    outs, rows = refs[2 * CHUNKS + 1 : -1], refs[-1]
    width = own[0].shape[1]
    for chunk in range(CHUNKS):
        rows[:, side(place[3] * CHUNKS + chunk, width)] = own[chunk][...]
        rows[:, side((1 - place[3]) * CHUNKS + chunk, width)] = arrived[chunk][...]
    for chunk in range(CHUNKS):
        for d in range(RING):
            for core in range(2):
                block = (lax.rem(place[0] + d, RING) * 2 + core) * CHUNKS + chunk
                outs[chunk * RING + d][:, core * width : (core + 1) * width] = jnp.dot(
                    rows[...], basis[:, side(block, width)], preferred_element_type=f32
                ).astype(bf16)


def moment_kernel(place, *refs):
    pieces, one, two = refs[:RING], refs[RING], refs[RING + 1]
    new_one, new_two, kept, lent = refs[-4:]
    core = pl.program_id(0)
    rotated = sum(piece[...].astype(f32) for piece in pieces)
    first = beta_first * one[...] + (1.0 - beta_first) * rotated
    second = beta_second * two[...] + (1.0 - beta_second) * rotated * rotated
    new_one[...] = first
    new_two[...] = second
    normed = (first / bias_first / (jnp.sqrt(second / bias_second) + epsilon)).astype(bf16)

    @pl.when(core == place[3])
    def _():
        kept[...] = normed

    @pl.when(core != place[3])
    def _():
        lent[...] = normed


def moments(place, chunk, pieces, one, two, so_far):
    rows, width = pieces[0].shape[0], pieces[0].shape[1] // 2
    piece = pl.BlockSpec((rows, width), lambda core, place: (0, core))
    part = pl.BlockSpec((rows, width), lambda core, place: (0, core * CHUNKS + chunk))
    whole = pl.BlockSpec((rows, width), lambda core, place: (0, 0))
    return pl.pallas_call(
        moment_kernel,
        out_shape=[shape(*one.shape, f32)] * 2 + [shape(rows, width)] * 2,
        grid_spec=pltpu.PrefetchScalarGridSpec(
            num_scalar_prefetch=1,
            grid=(2,),
            in_specs=[piece] * RING + [part, part] + [pl.BlockSpec(memory_space=pl.ANY)] * len(so_far),
            out_specs=[part, part, whole, whole],
        ),
        input_output_aliases={RING + 3: 0, RING + 4: 1} if so_far else {},
        compiler_params=pltpu.CompilerParams(vmem_limit_bytes=VMEM_LIMIT),
    )(place, *pieces, one, two, *so_far)


def back_kernel(place, *refs):
    pieces, left, left_other = refs[:RING], refs[RING], refs[RING + 1]
    outs, stack = refs[RING + 2 : 2 * RING + 2], refs[-1]
    chunk = pieces[0].shape[0]
    rows = chunk // 2
    for d in range(RING):
        stack[at(place[1] - d, chunk)] = pieces[d][...]
    for d in range(RING):
        lines = at(place[2] - d, rows)
        outs[d][:rows] = jnp.dot(left[lines], stack[...], preferred_element_type=f32).astype(bf16)
        outs[d][rows:] = jnp.dot(
            left_other[lines], stack[...], preferred_element_type=f32
        ).astype(bf16)


def beside_kernel(place, own, arrived, out):
    width = own.shape[1]
    out[:, side(place[3], width)] = own[...]
    out[:, side(1 - place[3], width)] = arrived[...]


def final_kernel(chunk, place, *refs):
    pieces, basis = refs[:RING], refs[RING]
    width = pieces[0].shape[1] // 2
    over = (((1,), (1,)), ((), ()))
    value = None
    for d in range(RING):
        for core in range(2):
            block = (lax.rem(place[0] - d + RING, RING) * 2 + core) * CHUNKS + chunk
            term = lax.dot_general(
                pieces[d][:, core * width : (core + 1) * width],
                basis[:, side(block, width)],
                over,
                preferred_element_type=f32,
            )
            value = term if value is None else value + term
    rest = refs[RING + 1 :]
    if chunk > 0:
        value = value + rest[0][...]
        rest = rest[1:]
    if chunk == CHUNKS - 1:
        weights, new_weights, update = rest
        update[...] = value
        new_weights[...] = weights[...] - learn_rate * (value + weight_decay * weights[...])
    else:
        rest[0][...] = value


def per_device(grad_parts, weights, moment_one, moment_two, left_basis, right_basis):
    place = jnp.stack([lax.axis_index(name) for name in ("x", "z", "y", "core")]).astype(jnp.int32)
    rows, features = left_basis.shape
    columns = weights.shape[1]
    half = columns // 2
    width = half // CHUNKS
    strip = features // RING
    both = 2 * rows

    (parts,) = call(strips_kernel, place, [left_basis], [jax.ShapeDtypeStruct((RING, rows, strip), bf16)])
    left = lax.all_to_all(parts, "y", 0, 0, tiled=True).reshape(RING * rows, strip)

    gradient = lax.psum_scatter(grad_parts[0], "x", scatter_dimension=1, tiled=True)
    (lent,) = call(lend_kernel, place, [gradient], [shape(rows, half)], after=[left])
    chunks = call(
        join_kernel, place, [gradient, swap(lent)], [shape(both, width)] * CHUNKS
    )
    basis = lax.all_gather(right_basis, ("z", "y", "core"), axis=0, tiled=True)

    left = held(left, chunks[:1])
    left_other = swap(left)

    kept, arrived = [], []
    for value in chunks:
        parts = call(
            left_kernel,
            place,
            [*gather(value, "y"), left, left_other],
            [shape(both, width)] * RING,
            4 * left.size * width,
            [pltpu.VMEM((RING * rows, width), bf16)] * 2,
        )
        own, other = call(
            functools.partial(sum_kernel, True), place, spread(parts, "z"), [shape(rows, width)] * 2
        )
        kept.append(own)
        arrived.append(swap(other))

    parts = call(
        right_kernel,
        place,
        [*kept, *arrived, basis],
        [shape(rows, 2 * width)] * (RING * CHUNKS),
        2 * rows * columns * RING * columns,
        [pltpu.VMEM((rows, columns), bf16)],
    )
    so_far, chunks = (), []
    for chunk in range(CHUNKS):
        pieces = spread(parts[chunk * RING : (chunk + 1) * RING], "x")
        *so_far, own, lent = moments(place, chunk, pieces, moment_one, moment_two, so_far)
        chunks.append(call(stack_kernel, place, [own, swap(lent)], [shape(both, width)])[0])
    new_one, new_two = so_far

    so_far = []
    for chunk, value in enumerate(chunks):
        parts = call(
            back_kernel,
            place,
            [*gather(value, "z"), left, left_other],
            [shape(both, width)] * RING,
            4 * left.size * width,
            [pltpu.VMEM((strip, width), bf16)],
        )
        own, other = call(
            functools.partial(sum_kernel, False), place, spread(parts, "y", -1), [shape(rows, width)] * 2
        )
        (value,) = call(beside_kernel, place, [own, swap(other)], [shape(rows, 2 * width)])
        last = chunk == CHUNKS - 1
        so_far = call(
            functools.partial(final_kernel, chunk),
            place,
            [*gather(value, "x"), basis, *so_far, *([weights] if last else [])],
            [shape(rows, columns, f32)] * (2 if last else 1),
            2 * rows * basis.size // CHUNKS,
        )
    new_weights, update = so_far
    return (new_weights, new_one, new_two, update)


def solution(mesh):
    grid = Mesh(mesh.devices.reshape(RING, RING, RING, 2), ("x", "z", "y", "core"))
    fsdp = ("z", "y", "core")
    placed = P(fsdp, "x")
    return jax.shard_map(
        per_device,
        mesh=grid,
        in_specs=(
            P("x", fsdp, None),
            placed,
            placed,
            placed,
            P(fsdp, None),
            P(("x", *fsdp), None),
        ),
        out_specs=(placed, placed, placed, placed),
        check_vma=False,
    )
```

```python
import functools

import jax
import jax.numpy as jnp
from jax import lax
from jax.experimental import pallas as pl
from jax.experimental.pallas import tpu as pltpu
from jax.sharding import Mesh, PartitionSpec as P

beta_first = 0.95
beta_second = 0.95
bias_first = 1.0 - 0.95**10
bias_second = 1.0 - 0.95**10
epsilon = 1e-08
learn_rate = 0.02
weight_decay = 0.1

RING = 4
CHUNKS = 2
bf16 = jnp.bfloat16
f32 = jnp.float32
VMEM_LIMIT = 40 * 1024 * 1024


def shift(value, axis, distance):
    return lax.ppermute(value, axis, [(i, (i + distance) % RING) for i in range(RING)])


def swap(value):
    return lax.ppermute(value, "core", [(0, 1), (1, 0)])


def gather(value, axis):
    return [value] + [shift(value, axis, d) for d in (1, 2, 3)]


def spread(parts, axis, sign=1):
    return [parts[0]] + [shift(parts[d], axis, sign * d) for d in (1, 2, 3)]


def shape(rows, columns, kind=bf16):
    return jax.ShapeDtypeStruct((rows, columns), kind)


def call(kernel, place, operands, outs, flops=0, scratch=(), after=()):
    def body(place, *refs):
        kernel(place, *refs[: len(operands)], *refs[len(operands) + len(after) :])

    moved = sum(a.size * a.dtype.itemsize for a in operands)
    moved += sum(s.size * jnp.dtype(s.dtype).itemsize for s in outs)
    return pl.pallas_call(
        body,
        out_shape=outs,
        in_specs=[pl.BlockSpec(memory_space=pltpu.SMEM)]
        + [pl.BlockSpec(memory_space=pltpu.VMEM)] * len(operands)
        + [pl.BlockSpec(memory_space=pl.ANY)] * len(after),
        out_specs=[pl.BlockSpec(memory_space=pltpu.VMEM)] * len(outs),
        scratch_shapes=list(scratch),
        cost_estimate=pl.CostEstimate(flops=flops, bytes_accessed=moved, transcendentals=0),
        compiler_params=pltpu.CompilerParams(vmem_limit_bytes=VMEM_LIMIT),
    )(place, *operands, *after)


def at(index, width):
    return pl.ds(pl.multiple_of(lax.rem(index + RING, RING) * width, width), width)


def side(which, width):
    return pl.ds(pl.multiple_of(which * width, width), width)


def strips_kernel(place, value, out):
    width = out.shape[2] // RING
    for k in range(RING):
        for j in range(RING):
            start = (j * RING + k) * width
            out[k, :, j * width : (j + 1) * width] = value[:, start : start + width]


def held(value, after):
    return pl.pallas_call(
        lambda *refs: None,
        out_shape=jax.ShapeDtypeStruct(value.shape, value.dtype),
        in_specs=[pl.BlockSpec(memory_space=pl.ANY)] * (1 + len(after)),
        out_specs=pl.BlockSpec(memory_space=pl.ANY),
        input_output_aliases={0: 0},
    )(value, *after)


def lend_kernel(place, value, out):
    out[...] = value[:, side(1 - place[3], out.shape[1])]


def join_kernel(place, value, arrived, *outs):
    rows, width = value.shape[0], outs[0].shape[1]
    for chunk, out in enumerate(outs):
        out[:rows] = value[:, side(place[3] * CHUNKS + chunk, width)]
        out[rows:] = arrived[:, chunk * width : (chunk + 1) * width]


def stack_kernel(place, own, arrived, out):
    rows = own.shape[0]
    out[side(place[3], rows)] = own[...]
    out[side(1 - place[3], rows)] = arrived[...]


def left_kernel(place, *refs):
    pieces, left, left_other = refs[:RING], refs[RING], refs[RING + 1]
    outs, stack, stack_other = refs[RING + 2 : 2 * RING + 2], refs[-2], refs[-1]
    rows, chunk = pieces[0].shape[0] // 2, outs[0].shape[0]
    for d in range(RING):
        stack[at(place[2] - d, rows)] = pieces[d][:rows]
        stack_other[at(place[2] - d, rows)] = pieces[d][rows:]
    over = (((0,), (0,)), ((), ()))
    for d in range(RING):
        columns = at(place[1] + d, chunk)
        value = lax.dot_general(stack[...], left[:, columns], over, preferred_element_type=f32)
        value += lax.dot_general(
            stack_other[...], left_other[:, columns], over, preferred_element_type=f32
        )
        outs[d][...] = value.T.astype(bf16)


def sum_kernel(absolute, place, *refs):
    pieces, own, other = refs[:RING], refs[RING], refs[RING + 1]
    rows = own.shape[0]
    for k, out in enumerate((own, other)):
        which = k + place[3] * (1 - 2 * k) if absolute else k
        lines = side(which, rows) if absolute else slice(k * rows, (k + 1) * rows)
        out[...] = sum(piece[lines].astype(f32) for piece in pieces).astype(bf16)


def right_kernel(chosen, place, *refs):
    own, arrived, basis = refs[:CHUNKS], refs[CHUNKS : 2 * CHUNKS], refs[2 * CHUNKS]
    outs, rows = refs[2 * CHUNKS + 1 : -1], refs[-1]
    width = own[0].shape[1]
    for chunk in range(CHUNKS):
        rows[:, side(place[3] * CHUNKS + chunk, width)] = own[chunk][...]
        rows[:, side((1 - place[3]) * CHUNKS + chunk, width)] = arrived[chunk][...]
    for d in range(RING):
        for core in range(2):
            block = (lax.rem(place[0] + d, RING) * 2 + core) * CHUNKS + chosen
            outs[d][:, core * width : (core + 1) * width] = jnp.dot(
                rows[...], basis[:, side(block, width)], preferred_element_type=f32
            ).astype(bf16)


def moment_kernel(place, *refs):
    pieces, one, two = refs[:RING], refs[RING], refs[RING + 1]
    new_one, new_two, kept, lent = refs[-4:]
    core = pl.program_id(0)
    rotated = sum(piece[...].astype(f32) for piece in pieces)
    first = beta_first * one[...] + (1.0 - beta_first) * rotated
    second = beta_second * two[...] + (1.0 - beta_second) * rotated * rotated
    new_one[...] = first
    new_two[...] = second
    normed = (first / bias_first / (jnp.sqrt(second / bias_second) + epsilon)).astype(bf16)

    @pl.when(core == place[3])
    def _():
        kept[...] = normed

    @pl.when(core != place[3])
    def _():
        lent[...] = normed


def moments(place, chunk, pieces, one, two, so_far):
    rows, width = pieces[0].shape[0], pieces[0].shape[1] // 2
    piece = pl.BlockSpec((rows, width), lambda core, place: (0, core))
    part = pl.BlockSpec((rows, width), lambda core, place: (0, core * CHUNKS + chunk))
    whole = pl.BlockSpec((rows, width), lambda core, place: (0, 0))
    return pl.pallas_call(
        moment_kernel,
        out_shape=[shape(*one.shape, f32)] * 2 + [shape(rows, width)] * 2,
        grid_spec=pltpu.PrefetchScalarGridSpec(
            num_scalar_prefetch=1,
            grid=(2,),
            in_specs=[piece] * RING + [part, part] + [pl.BlockSpec(memory_space=pl.ANY)] * len(so_far),
            out_specs=[part, part, whole, whole],
        ),
        input_output_aliases={RING + 3: 0, RING + 4: 1} if so_far else {},
        compiler_params=pltpu.CompilerParams(vmem_limit_bytes=VMEM_LIMIT),
    )(place, *pieces, one, two, *so_far)


def back_kernel(place, *refs):
    pieces, left, left_other = refs[:RING], refs[RING], refs[RING + 1]
    outs, stack = refs[RING + 2 : 2 * RING + 2], refs[-1]
    chunk = pieces[0].shape[0]
    rows = chunk // 2
    for d in range(RING):
        stack[at(place[1] - d, chunk)] = pieces[d][...]
    for d in range(RING):
        lines = at(place[2] - d, rows)
        outs[d][:rows] = jnp.dot(left[lines], stack[...], preferred_element_type=f32).astype(bf16)
        outs[d][rows:] = jnp.dot(
            left_other[lines], stack[...], preferred_element_type=f32
        ).astype(bf16)


def beside_kernel(place, own, arrived, out):
    width = own.shape[1]
    out[:, side(place[3], width)] = own[...]
    out[:, side(1 - place[3], width)] = arrived[...]


def final_kernel(chunk, place, *refs):
    pieces, basis = refs[:RING], refs[RING]
    width = pieces[0].shape[1] // 2
    over = (((1,), (1,)), ((), ()))
    value = None
    for d in range(RING):
        for core in range(2):
            block = (lax.rem(place[0] - d + RING, RING) * 2 + core) * CHUNKS + chunk
            term = lax.dot_general(
                pieces[d][:, core * width : (core + 1) * width],
                basis[:, side(block, width)],
                over,
                preferred_element_type=f32,
            )
            value = term if value is None else value + term
    rest = refs[RING + 1 :]
    if chunk > 0:
        value = value + rest[0][...]
        rest = rest[1:]
    if chunk == CHUNKS - 1:
        weights, new_weights, update = rest
        update[...] = value
        new_weights[...] = weights[...] - learn_rate * (value + weight_decay * weights[...])
    else:
        rest[0][...] = value


def per_device(grad_parts, weights, moment_one, moment_two, left_basis, right_basis):
    place = jnp.stack([lax.axis_index(name) for name in ("x", "z", "y", "core")]).astype(jnp.int32)
    rows, features = left_basis.shape
    columns = weights.shape[1]
    half = columns // 2
    width = half // CHUNKS
    strip = features // RING
    both = 2 * rows

    (parts,) = call(strips_kernel, place, [left_basis], [jax.ShapeDtypeStruct((RING, rows, strip), bf16)])
    left = lax.all_to_all(parts, "y", 0, 0, tiled=True).reshape(RING * rows, strip)

    gradient = lax.psum_scatter(grad_parts[0], "x", scatter_dimension=1, tiled=True)
    (lent,) = call(lend_kernel, place, [gradient], [shape(rows, half)], after=[left])
    chunks = call(
        join_kernel, place, [gradient, swap(lent)], [shape(both, width)] * CHUNKS
    )
    basis = lax.all_gather(right_basis, ("z", "y", "core"), axis=0, tiled=True)

    left = held(left, chunks[:1])
    left_other = swap(left)

    kept, arrived = [], []
    for value in chunks:
        parts = call(
            left_kernel,
            place,
            [*gather(value, "y"), left, left_other],
            [shape(both, width)] * RING,
            4 * left.size * width,
            [pltpu.VMEM((RING * rows, width), bf16)] * 2,
        )
        own, other = call(
            functools.partial(sum_kernel, True), place, spread(parts, "z"), [shape(rows, width)] * 2
        )
        kept.append(own)
        arrived.append(swap(other))

    so_far, chunks, follow = (), [], []
    for chunk in range(CHUNKS):
        parts = call(
            functools.partial(right_kernel, chunk),
            place,
            [*kept, *arrived, basis],
            [shape(rows, 2 * width)] * RING,
            2 * rows * columns * RING * columns // CHUNKS,
            [pltpu.VMEM((rows, columns), bf16)],
            after=follow,
        )
        follow = parts[:1]
        pieces = spread(parts, "x")
        *so_far, own, lent = moments(place, chunk, pieces, moment_one, moment_two, so_far)
        chunks.append(call(stack_kernel, place, [own, swap(lent)], [shape(both, width)])[0])
    new_one, new_two = so_far

    so_far = []
    for chunk, value in enumerate(chunks):
        parts = call(
            back_kernel,
            place,
            [*gather(value, "z"), left, left_other],
            [shape(both, width)] * RING,
            4 * left.size * width,
            [pltpu.VMEM((strip, width), bf16)],
        )
        own, other = call(
            functools.partial(sum_kernel, False), place, spread(parts, "y", -1), [shape(rows, width)] * 2
        )
        (value,) = call(beside_kernel, place, [own, swap(other)], [shape(rows, 2 * width)])
        last = chunk == CHUNKS - 1
        so_far = call(
            functools.partial(final_kernel, chunk),
            place,
            [*gather(value, "x"), basis, *so_far, *([weights] if last else [])],
            [shape(rows, columns, f32)] * (2 if last else 1),
            2 * rows * basis.size // CHUNKS,
        )
    new_weights, update = so_far
    return (new_weights, new_one, new_two, update)


def solution(mesh):
    grid = Mesh(mesh.devices.reshape(RING, RING, RING, 2), ("x", "z", "y", "core"))
    fsdp = ("z", "y", "core")
    placed = P(fsdp, "x")
    return jax.shard_map(
        per_device,
        mesh=grid,
        in_specs=(
            P("x", fsdp, None),
            placed,
            placed,
            placed,
            P(fsdp, None),
            P(("x", *fsdp), None),
        ),
        out_specs=(placed, placed, placed, placed),
        check_vma=False,
    )
```
